256 devices in a mesh: dom: 128 (over z, x, y_hi, core), col: 2 (over y_lo).
Axes of the slice: x: 4, y: 4 (y_hi: 2, y_lo: 2; y = y_hi * 2 + y_lo), z: 8, core: 2. Of those that a mesh axis runs over, the one named last changes fastest.
Arguments:
- density: bfloat16 [2, 768, 4, 128, 128], P(None, 'dom', 'col'), may hold values from -6 to 6
- hamiltonian: bfloat16 [768, 4, 128, 128], P('dom', 'col'), may hold values from -0.25 to 0.25
- neighbours: int32 [768, 4], P('dom'), may hold values from 0 to 767, as said below
Outputs:
- evolved: float32 [2, 768, 4, 128, 128], P(None, 'dom', 'col')
The draws below stay inside these ranges and needn't reach their ends.
Inputs may be any that keep to these rules, and one draw needn't show every extreme that they name: `neighbours`: each block row lists 4 different block rows, itself among them, none more than 3 rows away from it, in a drawn order of slots.
All inputs are finite; a program needn't handle non-finite values.
Results may differ from the reference program's by a relative error of at most 0.004.
Values may be sent and summed in bfloat16 or wider, within the bound.
No kernel may reach another device: no remote copies, remote signals or barrier semaphores. Data moves between devices by JAX's collectives and lax.ppermute only.
A program may use at most 64 MiB of HBM per device.

```python
import jax
import jax.numpy as jnp
from jax import lax

B = 128
K = 4
R = 6
STEPS = 2
ORDERS = 4
REACH = 3
NB = 768
N_DOM = 128


def draw_neighbours(key, part):
    first_key = jax.random.fold_in(key, 11)
    second_key = jax.random.fold_in(key, 23)
    window = 2 * REACH + 1
    offsets = jnp.arange(window, dtype=jnp.int32) - REACH
    candidates = jnp.arange(NB, dtype=jnp.int32)[:, None] + offsets[None, :]
    inside = (candidates >= 0) & (candidates < NB)
    scores = jax.random.randint(first_key, (NB, window), 0, 2 ** 20, dtype=jnp.int32) * 512 + jnp.arange(window, dtype=jnp.int32)[None, :]
    scores = jnp.where(offsets[None, :] == 0, 2 ** 30, scores)
    scores = jnp.where(inside, scores, -1)
    chosen = lax.top_k(scores, K)[1]
    picked = jnp.take_along_axis(candidates, chosen, axis=1)
    order_scores = jax.random.randint(second_key, (NB, K), 0, 2 ** 20, dtype=jnp.int32) * 64 + jnp.arange(K, dtype=jnp.int32)[None, :]
    slot_order = jnp.argsort(order_scores, axis=1, stable=True)
    return jnp.take_along_axis(picked, slot_order, axis=1).astype(jnp.int32)


def block_scale(key, shape, split, smallest, top_value):
    factor_of = 1.0
    for dim, blocks in split:
        draws = jax.random.uniform(jax.random.fold_in(jax.random.fold_in(key, 6), dim), (blocks,), jnp.float32, smallest / len(split), top_value / len(split))
        factor_of = factor_of * jnp.repeat(jnp.exp(draws), shape[dim] // blocks).reshape((-1,) + (1,) * (len(shape) - 1 - dim))
    return factor_of


def bell_draw(key, dims, scale, most, cuts=(), kind=jnp.bfloat16):
    array = scale * jax.random.normal(key, dims, jnp.float32)
    if cuts:
        array = array * block_scale(key, dims, cuts, -0.22, 0.18)
    return jnp.clip(array, -most, most).astype(kind)


def setup_inputs(seed: int = 0) -> dict:
    splits = jax.random.split(jax.random.key(seed), 4)
    return {
        "density": bell_draw(splits[0], (2, NB, K, B, B), 1.0, 6.0, ((1, 128), (2, 2))),
        "hamiltonian": bell_draw(splits[1], (NB, K, B, B), (K * B) ** -0.5, 0.25, ((0, 128), (1, 2))),
        "neighbours": draw_neighbours(jax.random.fold_in(splits[3], 71), 0),
    }


def commutator(hamiltonian, series_term, flat_index, present_mask):
    flat_term = series_term.reshape(2, NB * K, B, B)
    flat_operator = hamiltonian.reshape(NB * K, B, B)

    def domain_part(domain):
        first_row = (domain * R).astype(jnp.int32)
        index_rows = lax.dynamic_slice_in_dim(flat_index, first_row, R, 0)
        mask_rows = lax.dynamic_slice_in_dim(present_mask, first_row, R, 0)[..., None, None]
        picked_term = jnp.take(flat_term, index_rows, axis=1).astype(jnp.float32) * mask_rows
        picked_operator = jnp.take(flat_operator, index_rows, axis=0).astype(jnp.float32) * mask_rows
        operator_rows = lax.dynamic_slice_in_dim(hamiltonian, first_row, R, 0).astype(jnp.float32)
        term_rows = lax.dynamic_slice_in_dim(series_term, first_row, R, 1).astype(jnp.float32)
        left_product = jnp.einsum('rtab,zrstbc->zrsac', operator_rows, picked_term)
        right_product = jnp.einsum('zrtab,rstbc->zrsac', term_rows, picked_operator)
        return left_product - right_product

    pieces = lax.map(domain_part, jnp.arange(N_DOM, dtype=jnp.int32))
    return jnp.transpose(pieces, (1, 0, 2, 3, 4, 5)).reshape(2, NB, K, B, B)


def reference(density, hamiltonian, neighbours):
    rows_of = jnp.take(neighbours, neighbours, axis=0)
    matches = rows_of[:, None, :, :] == neighbours[:, :, None, None]
    present_mask = jnp.any(matches, axis=-1).astype(jnp.float32)
    slot_iota = jnp.arange(K, dtype=jnp.int32)
    slot_match = jnp.sum(jnp.where(matches, slot_iota, 0), axis=-1).astype(jnp.int32)
    flat_index = (neighbours[:, None, :] * K + slot_match).astype(jnp.int32)
    series_term = density
    running_sum = series_term.astype(jnp.float32)
    for time_step in range(STEPS):
        running_sum = series_term.astype(jnp.float32)
        for series_order in range(1, ORDERS + 1):
            bracket = commutator(hamiltonian, series_term, flat_index, present_mask)
            series_term = (jnp.stack([bracket[1], -bracket[0]]) / series_order).astype(jnp.bfloat16)
            series_term = lax.optimization_barrier(series_term)
            running_sum = running_sum + series_term.astype(jnp.float32)
        if time_step + 1 < STEPS:
            series_term = lax.optimization_barrier(running_sum.astype(jnp.bfloat16))
    return running_sum
```

```python
import functools

import jax
import jax.numpy as jnp
import numpy as np
from jax import lax
from jax.experimental import pallas as pl
from jax.experimental.pallas import tpu as pltpu
from jax.sharding import PartitionSpec as P

STEPS = 2
ORDERS = 4


def series_weights():
    factorial = [1]
    for n in range(1, STEPS * ORDERS + 1):
        factorial.append(factorial[-1] * n)
    once = [1.0 / factorial[n] for n in range(ORDERS + 1)]
    power = [1.0]
    for _ in range(STEPS):
        power = list(np.convolve(power, once))
    return [float(power[n] * factorial[n]) for n in range(STEPS * ORDERS + 1)]


WEIGHT = [(-1.0) ** (m // 2) * w for m, w in enumerate(series_weights())]
AXES = ("dom", "col")
ROWS = 6
SLOTS = 4
BLOCK = 128
HALF = ROWS * SLOTS // 2
OWN = ROWS * SLOTS
ZERO = 3 * OWN
TAB = 20


def flat_of(group, y, core):
    return ((group * 2 + y // 2) * 2 + core) * 2 + y % 2


def place_of(group, part, core, chain, groups):
    group = group % groups
    low = part ^ chain ^ (group % 2)
    return flat_of(group, chain * 2 + low, core)


def routes(groups):
    turn, keep, inner, outer = {}, {}, {}, {}
    left, right = {}, {}
    for group in range(groups):
        odd = group % 2
        for core in range(2):
            for y in range(4):
                here = flat_of(group, y, core)
                turn[here] = flat_of(group, (y + (1 if odd else 3)) % 4, core)
                stays = y % 2 == odd
                keep[here] = here if stays else flat_of(group, y ^ 2, core)
                inner[here] = flat_of(group, y, 1 - core)
                chain = y // 2
                part = chain ^ (y % 2) ^ odd
                ahead = (group, 1) if part == 0 else (group + 1, 0)
                behind = (group, 0) if part == 1 else (group - 1, 1)
                before = place_of(*behind, 1, chain, groups)
                after = place_of(*ahead, 0, chain, groups)
                outer[here] = after if core else before
                left[here] = inner[here] if core else before
                right[here] = after if core else inner[here]
    back = {target: source for source, target in turn.items()}
    pairs = lambda table: sorted(table.items())
    return {
        "turn": pairs(turn),
        "keep": pairs(keep),
        "turn_back": pairs(back),
        "keep_back": sorted((b, a) for a, b in keep.items()),
        "inner": pairs(inner),
        "outer": pairs(outer),
        "from_left": sorted((back[left[here]], here) for here in turn),
        "from_right": sorted((back[right[here]], here) for here in turn),
    }


def index_table(neighbours, route, group, core, chain, low, part):
    own = lax.ppermute(neighbours, AXES, route["turn"])
    left = lax.ppermute(neighbours, AXES, route["from_left"])
    right = lax.ppermute(neighbours, AXES, route["from_right"])
    left_low = jnp.where((core == 0) & (part == 1), 1 - low, low)
    right_low = jnp.where((core == 1) & (part == 0), 1 - low, low)
    turned = lambda lists, swap: jnp.where(swap == 1, jnp.roll(lists, 2, axis=1), lists)
    own, left, right = turned(own, low), turned(left, left_low), turned(right, right_low)
    first = (group * 4 + part * 2 + core - 1) * ROWS
    wide = jnp.concatenate([left, own, right], axis=0)
    lists = jnp.concatenate([own, left[3:], right[:3]], axis=0)
    where_rows = jnp.array(list(range(6, 12)) + [3, 4, 5, 12, 13, 14], jnp.int32)

    def flat(place, slot):
        side = place // ROWS
        row = place - side * ROWS
        outside = jnp.where((side == 0) == (core == 1), 0, 2)
        box = jnp.where(side == 1, 1, outside)
        return box * OWN + (slot // 2) * HALF + row * 2 + slot % 2

    place = lists - first
    inside = (place >= 0) & (place < 3 * ROWS)
    place = jnp.clip(place, 0, 3 * ROWS - 1)
    rows_of = jnp.take(wide, place, axis=0)
    matches = rows_of[:, None, :, :] == lists[:, :, None, None]
    present = jnp.any(matches, axis=-1) & inside[:, None, :]
    slot_iota = jnp.arange(SLOTS, dtype=jnp.int32)
    slot = jnp.sum(jnp.where(matches, slot_iota, 0), axis=-1)
    picked = jnp.where(present, flat(place[:, None, :], slot), ZERO)
    mine = flat(where_rows[:, None], slot_iota[None, :])
    table = jnp.concatenate([picked.reshape(-1, SLOTS * SLOTS), mine], axis=1)
    return jnp.concatenate([table.reshape(-1), chain[None]]).astype(jnp.int32)


def bracket(table, row, operator, term, inverse):
    at = lambda n: table[row * TAB + n]
    mine = [at(SLOTS * SLOTS + t) for t in range(SLOTS)]
    pick = [[at(s * SLOTS + t) for s in range(SLOTS)] for t in range(SLOTS)]
    wide = lambda ref, places: jnp.concatenate([ref[n] for n in places], axis=1)
    tall = lambda ref: jnp.concatenate([wide(ref, places) for places in pick], axis=0)
    left = jnp.dot(wide(operator, mine), tall(term), preferred_element_type=jnp.float32)
    right = jnp.dot(wide(term, mine), tall(operator), preferred_element_type=jnp.float32)
    fresh = ((left - right) * inverse).astype(jnp.bfloat16)
    return mine, [fresh[:, s * BLOCK : (s + 1) * BLOCK] for s in range(SLOTS)]


def two_orders(order, last, table, operator, own, inner, outer, *rest):
    if last:
        even_sum, odd_sum, kept, moved, term, first = rest
    else:
        first_out, second_out, term, first = rest
    zero = jnp.zeros((BLOCK, BLOCK), jnp.bfloat16)
    term[0:OWN] = inner[...]
    term[OWN : 2 * OWN] = own[...]
    term[2 * OWN : 3 * OWN] = outer[...]
    term[ZERO] = zero
    first[ZERO] = zero

    def first_row(row, carry):
        mine, blocks = bracket(table, row, operator, term, 1.0 / order)
        for n, block in zip(mine, blocks):
            first[n] = block
        return carry

    lax.fori_loop(0, 2 * ROWS, first_row, 0)

    if not last:
        first_out[...] = first[OWN : 2 * OWN]

    def second_row(row, carry):
        mine, blocks = bracket(table, row, operator, first, 1.0 / (order + 1))
        for n, block in zip(mine, blocks):
            if last:
                term[n] = block
            else:
                second_out[n - OWN] = block
        return carry

    lax.fori_loop(0, ROWS, second_row, 0)

    if last:
        chain = table[2 * ROWS * TAB]
        sign = jnp.where(chain == 0, -1.0, 1.0).astype(jnp.float32)

        def join(n, carry):
            for half, out in ((0, kept), (1, moved)):
                at = half * HALF + n
                even = even_sum[at] + WEIGHT[order + 1] * term[OWN + at].astype(jnp.float32)
                odd = odd_sum[at] + WEIGHT[order] * first[OWN + at].astype(jnp.float32)
                out[chain * HALF + n] = even.astype(jnp.bfloat16)
                out[(1 - chain) * HALF + n] = (sign * odd).astype(jnp.bfloat16)
            return carry

        lax.fori_loop(0, HALF, join, 0)


def run_orders(order, last, table, operator, own, inner, outer, sums=()):
    blocks = jax.ShapeDtypeStruct((OWN, BLOCK, BLOCK), jnp.bfloat16)
    vmem = pl.BlockSpec(memory_space=pltpu.VMEM)
    return pl.pallas_call(
        functools.partial(two_orders, order, last),
        out_shape=(blocks, blocks),
        in_specs=[pl.BlockSpec(memory_space=pltpu.SMEM)] + [vmem] * (4 + len(sums)),
        out_specs=(vmem, vmem),
        scratch_shapes=[pltpu.VMEM((ZERO + 1, BLOCK, BLOCK), jnp.bfloat16)] * 2,
        compiler_params=pltpu.CompilerParams(vmem_limit_bytes=32 * 1024 * 1024),
        cost_estimate=pl.CostEstimate(
            flops=18 * 2 * 2 * 128 * 512 * 512, bytes_accessed=6 * 2**20, transcendentals=0
        ),
        name="two_orders",
    )(table, operator, own, inner, outer, *sums)


def shards(groups, density, hamiltonian, neighbours):
    domain, low = lax.axis_index("dom"), lax.axis_index("col")
    route = routes(groups)
    group, chain, core = domain // 4, (domain // 2) % 2, domain % 2
    odd = group % 2
    part = chain ^ low ^ odd
    move = functools.partial(lax.ppermute, axis_name=AXES)

    own_h = hamiltonian.reshape(HALF, BLOCK, BLOCK)
    turn_part = chain ^ low ^ 1 ^ odd
    turn_x = lax.dynamic_index_in_dim(density, turn_part, 0, False).reshape(HALF, BLOCK, BLOCK)
    keep_x = lax.dynamic_index_in_dim(density, 1 - turn_part, 0, False).reshape(HALF, BLOCK, BLOCK)
    turn_h = move(own_h, perm=route["turn"])
    keep_h = move(own_h, perm=route["keep"])
    turn_x = move(turn_x, perm=route["turn"])
    keep_x = move(keep_x, perm=route["keep"])
    table = index_table(neighbours, route, group, core, chain, low, part)
    operator = jnp.concatenate([keep_h, turn_h], axis=0)
    operator = jnp.concatenate(
        [
            move(operator, perm=route["inner"]),
            operator,
            move(operator, perm=route["outer"]),
            jnp.zeros((1, BLOCK, BLOCK), jnp.bfloat16),
        ],
        axis=0,
    )
    term = jnp.concatenate([keep_x, turn_x], axis=0)
    sums = [term.astype(jnp.float32) * WEIGHT[0], jnp.zeros((), jnp.float32)]
    count = STEPS * ORDERS
    for order in range(1, count, 2):
        outer = move(term, perm=route["outer"])
        inner = move(term, perm=route["inner"])
        last = order + 1 == count
        first, term = run_orders(
            order, last, table, operator, term, inner, outer, tuple(sums) if last else ()
        )
        if not last:
            sums[1] = sums[1] + WEIGHT[order] * first.astype(jnp.float32)
            sums[0] = sums[0] + WEIGHT[order + 1] * term.astype(jnp.float32)
    kept = move(first, perm=route["keep_back"])
    moved = move(term, perm=route["turn_back"])
    total = kept.astype(jnp.float32) + moved.astype(jnp.float32)
    return total.reshape(density.shape)


def solution(mesh):
    placed = (P(None, "dom", "col", None, None), P("dom", "col", None, None), P("dom", None))
    return jax.shard_map(
        functools.partial(shards, mesh.shape["dom"] // 4),
        mesh=mesh,
        in_specs=placed,
        out_specs=P(None, "dom", "col", None, None),
        check_vma=False,
    )
```

```python
import functools

import jax
import jax.numpy as jnp
import numpy as np
from jax import lax
from jax.experimental import pallas as pl
from jax.experimental.pallas import tpu as pltpu
from jax.sharding import PartitionSpec as P

STEPS = 2
ORDERS = 4


def series_weights():
    factorial = [1]
    for n in range(1, STEPS * ORDERS + 1):
        factorial.append(factorial[-1] * n)
    once = [1.0 / factorial[n] for n in range(ORDERS + 1)]
    power = [1.0]
    for _ in range(STEPS):
        power = list(np.convolve(power, once))
    return [float(power[n] * factorial[n]) for n in range(STEPS * ORDERS + 1)]


WEIGHT = [(-1.0) ** (m // 2) * w for m, w in enumerate(series_weights())]
AXES = ("dom", "col")
ROWS = 6
SLOTS = 4
BLOCK = 128
HALF = ROWS * SLOTS // 2
OWN = ROWS * SLOTS
NEAR = 12
FAR = (0, 3, 5)
BOX = NEAR + 6
ZERO = 2 * BOX + OWN
TAB = 20
UNROLL = 6


def flat_of(group, y, core):
    return ((group * 2 + y // 2) * 2 + core) * 2 + y % 2


def place_of(group, part, core, chain, groups):
    group = group % groups
    low = part ^ chain ^ (group % 2)
    return flat_of(group, chain * 2 + low, core)


def routes(groups):
    turn, keep, relay, inner, outer = {}, {}, {}, {}, {}
    for group in range(groups):
        odd = group % 2
        for core in range(2):
            for y in range(4):
                here = flat_of(group, y, core)
                turn[here] = flat_of(group, (y + (1 if odd else 3)) % 4, core)
                relay[here] = flat_of(group, (y + (3 if odd else 1)) % 4, core)
                stays = y % 2 == odd
                keep[here] = here if stays else flat_of(group, y ^ 2, core)
                inner[here] = flat_of(group, y, 1 - core)
                chain = y // 2
                part = chain ^ (y % 2) ^ odd
                ahead = (group, 1) if part == 0 else (group + 1, 0)
                behind = (group, 0) if part == 1 else (group - 1, 1)
                before = place_of(*behind, 1, chain, groups)
                after = place_of(*ahead, 0, chain, groups)
                outer[here] = after if core else before
    back = {target: source for source, target in turn.items()}
    pairs = lambda table: sorted(table.items())
    return {
        "turn": pairs(turn),
        "keep": pairs(keep),
        "relay": pairs(relay),
        "turn_back": pairs(back),
        "keep_back": sorted((b, a) for a, b in keep.items()),
        "inner": pairs(inner),
        "outer": pairs(outer),
    }


def own_flat(row, slot):
    return (slot // 2) * HALF + row * 2 + slot % 2


def whereabouts():
    domain, low = lax.axis_index("dom"), lax.axis_index("col")
    group, chain, core = domain // 4, (domain // 2) % 2, domain % 2
    odd = group % 2
    part = chain ^ low ^ odd
    base = (group * 4 + part * 2 + core) * ROWS
    return group, chain, core, low, odd, part, base


TO_RIGHT = ((5, 4, 3), (2, 1, 0))
TO_LEFT = ((0, 1, 2), (3, 4, 5))


def make_pack(own, pack):
    _, chain, core, low, odd, _, base = whereabouts()
    for right, (near, far) in ((True, TO_RIGHT), (False, TO_LEFT)):
        start = (core if right else 1 - core) * BOX
        for n in range(NEAR):
            pack[start + n] = own_flat(near[n // SLOTS], n % SLOTS)
        for depth, row in enumerate(far):
            count = jnp.int32(0)
            for n in range(3 - depth):
                pack[start + NEAR + FAR[depth] + n] = own_flat(row, 0)
            for slot in range(SLOTS):
                place = own[row, slot ^ (2 * low)] - base
                wanted = place >= 3 if right else place <= 2
                spot = start + NEAR + FAR[depth] + count
                pack[jnp.where(wanted, spot, 2 * BOX + 2)] = own_flat(row, slot)
                count = count + wanted.astype(jnp.int32)
    pack[2 * BOX] = chain
    pack[2 * BOX + 1] = (low == odd).astype(jnp.int32)


def make_table(inner, own, outer, table, place, spot):
    _, _, core, low, _, part, base = whereabouts()
    left_low = jnp.where((core == 0) & (part == 1), 1 - low, low)
    right_low = jnp.where((core == 1) & (part == 0), 1 - low, low)
    first = base - ROWS
    for row in range(ROWS):
        for slot in range(SLOTS):
            at = (ROWS + row) * SLOTS + slot
            place[at] = own[row, slot ^ (2 * low)] - first
            spot[at] = BOX + own_flat(row, slot)
    sides = (
        (core == 1, left_low, 0, (1 - core) * (BOX + OWN), TO_RIGHT),
        (core == 0, right_low, 2 * ROWS, core * (BOX + OWN), TO_LEFT),
    )
    for inside, swap, offset, start, (near, far) in sides:
        for depth, row in enumerate(near + far):
            count = jnp.int32(0)
            for slot in range(SLOTS):
                at = (offset + row) * SLOTS + slot
                column = slot ^ (2 * swap)
                value = jnp.where(inside, inner[row, column], outer[row, column]) - first
                place[at] = value
                if depth < 3:
                    spot[at] = start + depth * SLOTS + slot
                else:
                    wanted = value <= 14 if offset else value >= 3
                    found = start + NEAR + FAR[depth - 3] + count
                    spot[at] = jnp.where(wanted, found, ZERO)
                    count = count + wanted.astype(jnp.int32)

    def fill(row, carry):
        here = jnp.where(row < 6, row + 6, jnp.where(row < 9, row - 3, row + 3)) * SLOTS
        lists = [place[here + n] for n in range(SLOTS)]
        for t in range(SLOTS):
            inside = (lists[t] >= 0) & (lists[t] < 3 * ROWS)
            there = jnp.clip(lists[t], 0, 3 * ROWS - 1) * SLOTS
            found = [(place[there + u], spot[there + u]) for u in range(SLOTS)]
            for s in range(SLOTS):
                index = jnp.int32(ZERO)
                for column, block in found:
                    index = jnp.where(inside & (column == lists[s]), block, index)
                table[row * TAB + s * SLOTS + t] = index
            table[row * TAB + SLOTS * SLOTS + t] = spot[here + t]
        return carry

    lax.fori_loop(0, 2 * ROWS, fill, 0)


def bracket(table, row, operator, term, inverse):
    at = lambda n: table[row * TAB + n]
    mine = [at(SLOTS * SLOTS + t) for t in range(SLOTS)]
    pick = [[at(s * SLOTS + t) for s in range(SLOTS)] for t in range(SLOTS)]
    wide = lambda ref, places: jnp.concatenate([ref[n] for n in places], axis=1)
    left = jnp.concatenate([wide(operator, mine), -wide(term, mine)], axis=1)
    right = jnp.concatenate([wide(ref, p) for ref in (term, operator) for p in pick], axis=0)
    fresh = jnp.dot(left, right, preferred_element_type=jnp.float32)
    fresh = (fresh * inverse).astype(jnp.bfloat16)
    return mine, [fresh[:, s * BLOCK : (s + 1) * BLOCK] for s in range(SLOTS)]


def send_blocks(pack, source, to_inner, to_outer):
    for n in range(BOX):
        to_inner[n] = source[pack[n]]
        to_outer[n] = source[pack[BOX + n]]


def assemble(choose, pack, *refs):
    if choose:
        here, kept, turned_in, own, to_inner, to_outer = refs

        @pl.when(pack[2 * BOX + 1] == 1)
        def _():
            own[0:HALF] = here[...]

        @pl.when(pack[2 * BOX + 1] == 0)
        def _():
            own[0:HALF] = kept[...]

    else:
        kept, turned_in, own, to_inner, to_outer = refs
        own[0:HALF] = kept[...]
    own[HALF:OWN] = turned_in[...]
    send_blocks(pack, own, to_inner, to_outer)


def two_orders(order, last, table, pack, operator, own, inner, outer, *rest):
    if last:
        even_sum, odd_sum, kept, moved, term, first = rest
    else:
        first_out, second_out, to_inner, to_outer, term, first = rest
    zero = jnp.zeros((BLOCK, BLOCK), jnp.bfloat16)
    term[0:BOX] = inner[...]
    term[BOX : BOX + OWN] = own[...]
    term[BOX + OWN : ZERO] = outer[...]
    term[ZERO] = zero
    first[ZERO] = zero

    def first_row(row, carry):
        mine, blocks = bracket(table, row, operator, term, 1.0 / order)
        for n, block in zip(mine, blocks):
            first[n] = block
        return carry

    lax.fori_loop(0, 2 * ROWS, first_row, 0, unroll=UNROLL)

    if not last:
        first_out[...] = first[BOX : BOX + OWN]

    def second_row(row, carry):
        mine, blocks = bracket(table, row, operator, first, 1.0 / (order + 1))
        for n, block in zip(mine, blocks):
            if last:
                term[n] = block
            else:
                second_out[n - BOX] = block
        return carry

    lax.fori_loop(0, ROWS, second_row, 0, unroll=UNROLL)

    if not last:
        send_blocks(pack, second_out, to_inner, to_outer)
    else:
        chain = pack[2 * BOX]
        sign = jnp.where(chain == 0, -1.0, 1.0).astype(jnp.float32)

        def join(n, carry):
            for half, out in ((0, kept), (1, moved)):
                at = half * HALF + n
                even = even_sum[at] + WEIGHT[order + 1] * term[BOX + at].astype(jnp.float32)
                odd = odd_sum[at] + WEIGHT[order] * first[BOX + at].astype(jnp.float32)
                out[chain * HALF + n] = even.astype(jnp.bfloat16)
                out[(1 - chain) * HALF + n] = (sign * odd).astype(jnp.bfloat16)
            return carry

        lax.fori_loop(0, HALF, join, 0, unroll=4)


VMEM = pl.BlockSpec(memory_space=pltpu.VMEM)
SMEM = pl.BlockSpec(memory_space=pltpu.SMEM)


def blocks_of(count):
    return jax.ShapeDtypeStruct((count, BLOCK, BLOCK), jnp.bfloat16)


def run_pack(own):
    return pl.pallas_call(
        make_pack,
        out_shape=jax.ShapeDtypeStruct((2 * BOX + 3,), jnp.int32),
        in_specs=[SMEM],
        out_specs=SMEM,
        cost_estimate=pl.CostEstimate(flops=10**6, bytes_accessed=1024, transcendentals=0),
        name="make_pack",
    )(own)


def run_table(left, own, right):
    return pl.pallas_call(
        make_table,
        out_shape=jax.ShapeDtypeStruct((2 * ROWS * TAB,), jnp.int32),
        in_specs=[SMEM] * 3,
        out_specs=SMEM,
        scratch_shapes=[pltpu.SMEM((3 * ROWS * SLOTS,), jnp.int32)] * 2,
        cost_estimate=pl.CostEstimate(flops=10**6, bytes_accessed=1024, transcendentals=0),
        name="make_table",
    )(left, own, right)


def run_assemble(choose, pack, *pieces):
    return pl.pallas_call(
        functools.partial(assemble, choose),
        out_shape=(blocks_of(OWN), blocks_of(BOX), blocks_of(BOX)),
        in_specs=[SMEM] + [VMEM] * len(pieces),
        out_specs=(VMEM,) * 3,
        compiler_params=pltpu.CompilerParams(vmem_limit_bytes=16 * 1024 * 1024),
        cost_estimate=pl.CostEstimate(flops=0, bytes_accessed=3 * 2**20, transcendentals=0),
        name="assemble",
    )(pack, *pieces)


def run_orders(order, last, table, pack, operator, own, inner, outer, sums=()):
    sizes = (OWN, OWN) if last else (OWN, OWN, BOX, BOX)
    return pl.pallas_call(
        functools.partial(two_orders, order, last),
        out_shape=tuple(blocks_of(size) for size in sizes),
        in_specs=[SMEM] * 2 + [VMEM] * (4 + len(sums)),
        out_specs=(VMEM,) * len(sizes),
        scratch_shapes=[pltpu.VMEM((ZERO + 1, BLOCK, BLOCK), jnp.bfloat16)] * 2,
        compiler_params=pltpu.CompilerParams(vmem_limit_bytes=32 * 1024 * 1024),
        cost_estimate=pl.CostEstimate(
            flops=18 * 2 * 2 * 128 * 512 * 512, bytes_accessed=6 * 2**20, transcendentals=0
        ),
        name="two_orders",
    )(table, pack, operator, own, inner, outer, *sums)


def shards(groups, density, hamiltonian, neighbours):
    route = routes(groups)
    _, chain, _, low, odd, _, _ = whereabouts()
    move = functools.partial(lax.ppermute, axis_name=AXES)

    own_h = hamiltonian.reshape(HALF, BLOCK, BLOCK)
    own_lists = move(neighbours, perm=route["turn"])
    own_h, own_lists = lax.optimization_barrier((own_h, own_lists))
    first_side = move(own_lists, perm=route["inner"])
    second_side = move(own_lists, perm=route["outer"])
    turn_h = move(own_h, perm=route["turn"])
    keep_h = move(own_h, perm=route["keep"])
    turn_part = chain ^ low ^ 1 ^ odd
    turn_x = lax.dynamic_index_in_dim(density, turn_part, 0, False).reshape(HALF, BLOCK, BLOCK)
    here_x = lax.dynamic_index_in_dim(density, 1 - turn_part, 0, False).reshape(HALF, BLOCK, BLOCK)
    keep_x = move(here_x, perm=route["relay"])
    turn_x = move(turn_x, perm=route["turn"])
    keep_x = move(keep_x, perm=route["relay"])

    pack = run_pack(own_lists)
    operator, to_inner, to_outer = run_assemble(False, pack, keep_h, turn_h)
    table = run_table(first_side, own_lists, second_side)
    to_inner, to_outer, first_side, second_side = lax.optimization_barrier(
        (to_inner, to_outer, first_side, second_side)
    )
    outer = move(to_outer, perm=route["outer"])
    inner = move(to_inner, perm=route["inner"])
    zero = jnp.zeros((1, BLOCK, BLOCK), jnp.bfloat16)
    operator = jnp.concatenate([inner, operator, outer, zero], axis=0)

    term, to_inner, to_outer = run_assemble(True, pack, here_x, keep_x, turn_x)
    sums = [term.astype(jnp.float32) * WEIGHT[0], jnp.zeros((), jnp.float32)]
    count = STEPS * ORDERS
    for order in range(1, count, 2):
        outer = move(to_outer, perm=route["outer"])
        inner = move(to_inner, perm=route["inner"])
        if order + 1 == count:
            break
        first, term, to_inner, to_outer = run_orders(
            order, False, table, pack, operator, term, inner, outer
        )
        sums[1] = sums[1] + WEIGHT[order] * first.astype(jnp.float32)
        sums[0] = sums[0] + WEIGHT[order + 1] * term.astype(jnp.float32)
    kept, moved = run_orders(
        count - 1, True, table, pack, operator, term, inner, outer, tuple(sums)
    )
    kept = move(kept, perm=route["keep_back"])
    moved = move(moved, perm=route["turn_back"])
    total = kept.astype(jnp.float32) + moved.astype(jnp.float32)
    return total.reshape(density.shape)


def solution(mesh):
    placed = (P(None, "dom", "col", None, None), P("dom", "col", None, None), P("dom", None))
    return jax.shard_map(
        functools.partial(shards, mesh.shape["dom"] // 4),
        mesh=mesh,
        in_specs=placed,
        out_specs=P(None, "dom", "col", None, None),
        check_vma=False,
    )
```

```python
import functools

import jax
import jax.numpy as jnp
import numpy as np
from jax import lax
from jax.experimental import pallas as pl
from jax.experimental.pallas import tpu as pltpu
from jax.sharding import PartitionSpec as P

STEPS = 2
ORDERS = 4


def series_weights():
    factorial = [1]
    for n in range(1, STEPS * ORDERS + 1):
        factorial.append(factorial[-1] * n)
    once = [1.0 / factorial[n] for n in range(ORDERS + 1)]
    power = [1.0]
    for _ in range(STEPS):
        power = list(np.convolve(power, once))
    return [float(power[n] * factorial[n]) for n in range(STEPS * ORDERS + 1)]


WEIGHT = [(-1.0) ** (m // 2) * w for m, w in enumerate(series_weights())]
AXES = ("dom", "col")
ROWS = 6
SLOTS = 4
BLOCK = 128
HALF = ROWS * SLOTS // 2
OWN = ROWS * SLOTS
NEAR = 12
FAR = (0, 3, 5)
BOX = NEAR + 6
ZERO = 2 * BOX + OWN
TAB = 20
UNROLL = 12


def flat_of(group, y, core):
    return ((group * 2 + y // 2) * 2 + core) * 2 + y % 2


def place_of(group, part, core, chain, groups):
    group = group % groups
    low = part ^ chain ^ (group % 2)
    return flat_of(group, chain * 2 + low, core)


def routes(groups):
    turn, keep, relay, inner, outer = {}, {}, {}, {}, {}
    for group in range(groups):
        odd = group % 2
        for core in range(2):
            for y in range(4):
                here = flat_of(group, y, core)
                turn[here] = flat_of(group, (y + (1 if odd else 3)) % 4, core)
                relay[here] = flat_of(group, (y + (3 if odd else 1)) % 4, core)
                stays = y % 2 == odd
                keep[here] = here if stays else flat_of(group, y ^ 2, core)
                inner[here] = flat_of(group, y, 1 - core)
                chain = y // 2
                part = chain ^ (y % 2) ^ odd
                ahead = (group, 1) if part == 0 else (group + 1, 0)
                behind = (group, 0) if part == 1 else (group - 1, 1)
                before = place_of(*behind, 1, chain, groups)
                after = place_of(*ahead, 0, chain, groups)
                outer[here] = after if core else before
    back = {target: source for source, target in turn.items()}
    pairs = lambda table: sorted(table.items())
    return {
        "turn": pairs(turn),
        "keep": pairs(keep),
        "relay": pairs(relay),
        "turn_back": pairs(back),
        "keep_back": sorted((b, a) for a, b in keep.items()),
        "inner": pairs(inner),
        "outer": pairs(outer),
    }


def own_flat(row, slot):
    return (slot // 2) * HALF + row * 2 + slot % 2


def whereabouts():
    domain, low = lax.axis_index("dom"), lax.axis_index("col")
    group, chain, core = domain // 4, (domain // 2) % 2, domain % 2
    odd = group % 2
    part = chain ^ low ^ odd
    base = (group * 4 + part * 2 + core) * ROWS
    return group, chain, core, low, odd, part, base


TO_RIGHT = ((5, 4, 3), (2, 1, 0))
TO_LEFT = ((0, 1, 2), (3, 4, 5))


def make_pack(own, pack):
    _, chain, core, low, odd, _, base = whereabouts()
    for right, (near, far) in ((True, TO_RIGHT), (False, TO_LEFT)):
        start = (core if right else 1 - core) * BOX
        for n in range(NEAR):
            pack[start + n] = own_flat(near[n // SLOTS], n % SLOTS)
        for depth, row in enumerate(far):
            count = jnp.int32(0)
            for n in range(3 - depth):
                pack[start + NEAR + FAR[depth] + n] = own_flat(row, 0)
            for slot in range(SLOTS):
                place = own[row, slot ^ (2 * low)] - base
                wanted = place >= 3 if right else place <= 2
                spot = start + NEAR + FAR[depth] + count
                pack[jnp.where(wanted, spot, 2 * BOX + 2)] = own_flat(row, slot)
                count = count + wanted.astype(jnp.int32)
    pack[2 * BOX] = chain
    pack[2 * BOX + 1] = (low == odd).astype(jnp.int32)


def make_table(inner, own, outer, table, place, spot):
    _, _, core, low, _, part, base = whereabouts()
    left_low = jnp.where((core == 0) & (part == 1), 1 - low, low)
    right_low = jnp.where((core == 1) & (part == 0), 1 - low, low)
    first = base - ROWS
    for row in range(ROWS):
        for slot in range(SLOTS):
            at = (ROWS + row) * SLOTS + slot
            place[at] = own[row, slot ^ (2 * low)] - first
            spot[at] = BOX + own_flat(row, slot)
    sides = (
        (core == 1, left_low, 0, (1 - core) * (BOX + OWN), TO_RIGHT),
        (core == 0, right_low, 2 * ROWS, core * (BOX + OWN), TO_LEFT),
    )
    for inside, swap, offset, start, (near, far) in sides:
        for depth, row in enumerate(near + far):
            count = jnp.int32(0)
            for slot in range(SLOTS):
                at = (offset + row) * SLOTS + slot
                column = slot ^ (2 * swap)
                value = jnp.where(inside, inner[row, column], outer[row, column]) - first
                place[at] = value
                if depth < 3:
                    spot[at] = start + depth * SLOTS + slot
                else:
                    wanted = value <= 14 if offset else value >= 3
                    found = start + NEAR + FAR[depth - 3] + count
                    spot[at] = jnp.where(wanted, found, ZERO)
                    count = count + wanted.astype(jnp.int32)

    def fill(row, carry):
        here = jnp.where(row < 6, row + 6, jnp.where(row < 9, row - 3, row + 3)) * SLOTS
        lists = [place[here + n] for n in range(SLOTS)]
        for t in range(SLOTS):
            inside = (lists[t] >= 0) & (lists[t] < 3 * ROWS)
            there = jnp.clip(lists[t], 0, 3 * ROWS - 1) * SLOTS
            found = [(place[there + u], spot[there + u]) for u in range(SLOTS)]
            for s in range(SLOTS):
                index = jnp.int32(ZERO)
                for column, block in found:
                    index = jnp.where(inside & (column == lists[s]), block, index)
                table[row * TAB + s * SLOTS + t] = index
            table[row * TAB + SLOTS * SLOTS + t] = spot[here + t]
        return carry

    lax.fori_loop(0, 2 * ROWS, fill, 0)


def bracket(table, row, operator, term, inverse):
    at = lambda n: table[row * TAB + n]
    mine = [at(SLOTS * SLOTS + t) for t in range(SLOTS)]
    pick = [[at(s * SLOTS + t) for s in range(SLOTS)] for t in range(SLOTS)]
    wide = lambda ref, places: jnp.concatenate([ref[n] for n in places], axis=1)
    left = jnp.concatenate([wide(operator, mine), -wide(term, mine)], axis=1)
    right = jnp.concatenate([wide(ref, p) for ref in (term, operator) for p in pick], axis=0)
    fresh = jnp.dot(left, right, preferred_element_type=jnp.float32)
    fresh = (fresh * inverse).astype(jnp.bfloat16)
    return mine, [fresh[:, s * BLOCK : (s + 1) * BLOCK] for s in range(SLOTS)]


def send_blocks(pack, source, to_inner, to_outer):
    for n in range(BOX):
        to_inner[n] = source[pack[n]]
        to_outer[n] = source[pack[BOX + n]]


def assemble(choose, pack, *refs):
    if choose:
        here, kept, turned_in, own, to_inner, to_outer = refs

        @pl.when(pack[2 * BOX + 1] == 1)
        def _():
            own[0:HALF] = here[...]

        @pl.when(pack[2 * BOX + 1] == 0)
        def _():
            own[0:HALF] = kept[...]

    else:
        kept, turned_in, own, to_inner, to_outer = refs
        own[0:HALF] = kept[...]
    own[HALF:OWN] = turned_in[...]
    send_blocks(pack, own, to_inner, to_outer)


def two_orders(order, last, table, pack, operator, own, inner, outer, *rest):
    if last:
        even_sum, odd_sum, kept, moved, term, first = rest
    else:
        first_out, second_out, to_inner, to_outer, term, first = rest
    zero = jnp.zeros((BLOCK, BLOCK), jnp.bfloat16)
    term[0:BOX] = inner[...]
    term[BOX : BOX + OWN] = own[...]
    term[BOX + OWN : ZERO] = outer[...]
    term[ZERO] = zero
    first[ZERO] = zero

    def first_row(row, carry):
        mine, blocks = bracket(table, row, operator, term, 1.0 / order)
        for n, block in zip(mine, blocks):
            first[n] = block
        return carry

    lax.fori_loop(0, 2 * ROWS, first_row, 0, unroll=UNROLL)

    if not last:
        first_out[...] = first[BOX : BOX + OWN]

    def second_row(row, carry):
        mine, blocks = bracket(table, row, operator, first, 1.0 / (order + 1))
        for n, block in zip(mine, blocks):
            if last:
                term[n] = block
            else:
                second_out[n - BOX] = block
        return carry

    lax.fori_loop(0, ROWS, second_row, 0, unroll=ROWS)

    if not last:
        send_blocks(pack, second_out, to_inner, to_outer)
    else:
        chain = pack[2 * BOX]
        sign = jnp.where(chain == 0, -1.0, 1.0).astype(jnp.float32)

        def join(n, carry):
            for half, out in ((0, kept), (1, moved)):
                at = half * HALF + n
                even = even_sum[at] + WEIGHT[order + 1] * term[BOX + at].astype(jnp.float32)
                odd = odd_sum[at] + WEIGHT[order] * first[BOX + at].astype(jnp.float32)
                out[chain * HALF + n] = even.astype(jnp.bfloat16)
                out[(1 - chain) * HALF + n] = (sign * odd).astype(jnp.bfloat16)
            return carry

        lax.fori_loop(0, HALF, join, 0, unroll=4)


VMEM = pl.BlockSpec(memory_space=pltpu.VMEM)
SMEM = pl.BlockSpec(memory_space=pltpu.SMEM)


def blocks_of(count):
    return jax.ShapeDtypeStruct((count, BLOCK, BLOCK), jnp.bfloat16)


def run_pack(own):
    return pl.pallas_call(
        make_pack,
        out_shape=jax.ShapeDtypeStruct((2 * BOX + 3,), jnp.int32),
        in_specs=[SMEM],
        out_specs=SMEM,
        cost_estimate=pl.CostEstimate(flops=10**6, bytes_accessed=1024, transcendentals=0),
        name="make_pack",
    )(own)


def run_table(left, own, right):
    return pl.pallas_call(
        make_table,
        out_shape=jax.ShapeDtypeStruct((2 * ROWS * TAB,), jnp.int32),
        in_specs=[SMEM] * 3,
        out_specs=SMEM,
        scratch_shapes=[pltpu.SMEM((3 * ROWS * SLOTS,), jnp.int32)] * 2,
        cost_estimate=pl.CostEstimate(flops=10**6, bytes_accessed=1024, transcendentals=0),
        name="make_table",
    )(left, own, right)


def run_assemble(choose, pack, *pieces):
    return pl.pallas_call(
        functools.partial(assemble, choose),
        out_shape=(blocks_of(OWN), blocks_of(BOX), blocks_of(BOX)),
        in_specs=[SMEM] + [VMEM] * len(pieces),
        out_specs=(VMEM,) * 3,
        compiler_params=pltpu.CompilerParams(vmem_limit_bytes=16 * 1024 * 1024),
        cost_estimate=pl.CostEstimate(flops=0, bytes_accessed=3 * 2**20, transcendentals=0),
        name="assemble",
    )(pack, *pieces)


def run_orders(order, last, table, pack, operator, own, inner, outer, sums=()):
    sizes = (OWN, OWN) if last else (OWN, OWN, BOX, BOX)
    return pl.pallas_call(
        functools.partial(two_orders, order, last),
        out_shape=tuple(blocks_of(size) for size in sizes),
        in_specs=[SMEM] * 2 + [VMEM] * (4 + len(sums)),
        out_specs=(VMEM,) * len(sizes),
        scratch_shapes=[pltpu.VMEM((ZERO + 1, BLOCK, BLOCK), jnp.bfloat16)] * 2,
        compiler_params=pltpu.CompilerParams(vmem_limit_bytes=32 * 1024 * 1024),
        cost_estimate=pl.CostEstimate(
            flops=18 * 2 * 2 * 128 * 512 * 512, bytes_accessed=6 * 2**20, transcendentals=0
        ),
        name="two_orders",
    )(table, pack, operator, own, inner, outer, *sums)


def shards(groups, density, hamiltonian, neighbours):
    route = routes(groups)
    _, chain, _, low, odd, _, _ = whereabouts()
    move = functools.partial(lax.ppermute, axis_name=AXES)

    own_h = hamiltonian.reshape(HALF, BLOCK, BLOCK)
    own_lists = move(neighbours, perm=route["turn"])
    turn_part = chain ^ low ^ 1 ^ odd
    own_h, own_lists, turn_part = lax.optimization_barrier((own_h, own_lists, turn_part))
    first_side = move(own_lists, perm=route["inner"])
    second_side = move(own_lists, perm=route["outer"])
    turn_h = move(own_h, perm=route["turn"])
    keep_h = move(own_h, perm=route["keep"])
    turn_x = lax.dynamic_index_in_dim(density, turn_part, 0, False).reshape(HALF, BLOCK, BLOCK)
    here_x = lax.dynamic_index_in_dim(density, 1 - turn_part, 0, False).reshape(HALF, BLOCK, BLOCK)
    keep_x = move(here_x, perm=route["relay"])
    turn_x = move(turn_x, perm=route["turn"])
    keep_x = move(keep_x, perm=route["relay"])

    pack = run_pack(own_lists)
    operator, to_inner, to_outer = run_assemble(False, pack, keep_h, turn_h)
    table = run_table(first_side, own_lists, second_side)
    to_inner, to_outer, first_side, second_side = lax.optimization_barrier(
        (to_inner, to_outer, first_side, second_side)
    )
    outer = move(to_outer, perm=route["outer"])
    inner = move(to_inner, perm=route["inner"])
    zero = jnp.zeros((1, BLOCK, BLOCK), jnp.bfloat16)
    operator = jnp.concatenate([inner, operator, outer, zero], axis=0)

    term, to_inner, to_outer = run_assemble(True, pack, here_x, keep_x, turn_x)
    sums = [term.astype(jnp.float32) * WEIGHT[0], jnp.zeros((), jnp.float32)]
    count = STEPS * ORDERS
    for order in range(1, count, 2):
        outer = move(to_outer, perm=route["outer"])
        inner = move(to_inner, perm=route["inner"])
        if order + 1 == count:
            break
        first, term, to_inner, to_outer = run_orders(
            order, False, table, pack, operator, term, inner, outer
        )
        sums[1] = sums[1] + WEIGHT[order] * first.astype(jnp.float32)
        sums[0] = sums[0] + WEIGHT[order + 1] * term.astype(jnp.float32)
    kept, moved = run_orders(
        count - 1, True, table, pack, operator, term, inner, outer, tuple(sums)
    )
    kept = move(kept, perm=route["keep_back"])
    moved = move(moved, perm=route["turn_back"])
    total = kept.astype(jnp.float32) + moved.astype(jnp.float32)
    return total.reshape(density.shape)


def solution(mesh):
    placed = (P(None, "dom", "col", None, None), P("dom", "col", None, None), P("dom", None))
    return jax.shard_map(
        functools.partial(shards, mesh.shape["dom"] // 4),
        mesh=mesh,
        in_specs=placed,
        out_specs=P(None, "dom", "col", None, None),
        check_vma=False,
    )
```

```python
import functools

import jax
import jax.numpy as jnp
import numpy as np
from jax import lax
from jax.experimental import pallas as pl
from jax.experimental.pallas import tpu as pltpu
from jax.sharding import PartitionSpec as P

STEPS = 2
ORDERS = 4


def series_weights():
    factorial = [1]
    for n in range(1, STEPS * ORDERS + 1):
        factorial.append(factorial[-1] * n)
    once = [1.0 / factorial[n] for n in range(ORDERS + 1)]
    power = [1.0]
    for _ in range(STEPS):
        power = list(np.convolve(power, once))
    return [float(power[n] * factorial[n]) for n in range(STEPS * ORDERS + 1)]


WEIGHT = [(-1.0) ** (m // 2) * w for m, w in enumerate(series_weights())]
AXES = ("dom", "col")
ROWS = 6
SLOTS = 4
BLOCK = 128
HALF = ROWS * SLOTS // 2
OWN = ROWS * SLOTS
NEAR = 12
FAR = (0, 3, 5)
BOX = NEAR + 6
ZERO = 2 * BOX + OWN
TAB = 20
UNROLL = 12


def flat_of(group, y, core):
    return ((group * 2 + y // 2) * 2 + core) * 2 + y % 2


def place_of(group, part, core, chain, groups):
    group = group % groups
    low = part ^ chain ^ (group % 2)
    return flat_of(group, chain * 2 + low, core)


def routes(groups):
    turn, keep, relay, inner, outer = {}, {}, {}, {}, {}
    for group in range(groups):
        odd = group % 2
        for core in range(2):
            for y in range(4):
                here = flat_of(group, y, core)
                turn[here] = flat_of(group, (y + (1 if odd else 3)) % 4, core)
                relay[here] = flat_of(group, (y + (3 if odd else 1)) % 4, core)
                stays = y % 2 == odd
                keep[here] = here if stays else flat_of(group, y ^ 2, core)
                inner[here] = flat_of(group, y, 1 - core)
                chain = y // 2
                part = chain ^ (y % 2) ^ odd
                ahead = (group, 1) if part == 0 else (group + 1, 0)
                behind = (group, 0) if part == 1 else (group - 1, 1)
                before = place_of(*behind, 1, chain, groups)
                after = place_of(*ahead, 0, chain, groups)
                outer[here] = after if core else before
    back = {target: source for source, target in turn.items()}
    pairs = lambda table: sorted(table.items())
    return {
        "turn": pairs(turn),
        "keep": pairs(keep),
        "relay": pairs(relay),
        "turn_back": pairs(back),
        "keep_back": sorted((b, a) for a, b in keep.items()),
        "inner": pairs(inner),
        "outer": pairs(outer),
    }


def own_flat(row, slot):
    return (slot // 2) * HALF + row * 2 + slot % 2


def whereabouts():
    domain, low = lax.axis_index("dom"), lax.axis_index("col")
    group, chain, core = domain // 4, (domain // 2) % 2, domain % 2
    odd = group % 2
    part = chain ^ low ^ odd
    base = (group * 4 + part * 2 + core) * ROWS
    return group, chain, core, low, odd, part, base


TO_RIGHT = ((5, 4, 3), (2, 1, 0))
TO_LEFT = ((0, 1, 2), (3, 4, 5))


def make_pack(own, pack):
    _, chain, core, low, odd, _, base = whereabouts()
    for right, (near, far) in ((True, TO_RIGHT), (False, TO_LEFT)):
        start = (core if right else 1 - core) * BOX
        for n in range(NEAR):
            pack[start + n] = own_flat(near[n // SLOTS], n % SLOTS)
        for depth, row in enumerate(far):
            count = jnp.int32(0)
            for n in range(3 - depth):
                pack[start + NEAR + FAR[depth] + n] = own_flat(row, 0)
            for slot in range(SLOTS):
                place = own[row, slot ^ (2 * low)] - base
                wanted = place >= 3 if right else place <= 2
                spot = start + NEAR + FAR[depth] + count
                pack[jnp.where(wanted, spot, 2 * BOX + 2)] = own_flat(row, slot)
                count = count + wanted.astype(jnp.int32)
    pack[2 * BOX] = chain
    pack[2 * BOX + 1] = (low == odd).astype(jnp.int32)


def make_table(inner, own, outer, table, place, spot):
    _, _, core, low, _, part, base = whereabouts()
    left_low = jnp.where((core == 0) & (part == 1), 1 - low, low)
    right_low = jnp.where((core == 1) & (part == 0), 1 - low, low)
    first = base - ROWS
    for row in range(ROWS):
        for slot in range(SLOTS):
            at = (ROWS + row) * SLOTS + slot
            place[at] = own[row, slot ^ (2 * low)] - first
            spot[at] = BOX + own_flat(row, slot)
    sides = (
        (core == 1, left_low, 0, (1 - core) * (BOX + OWN), TO_RIGHT),
        (core == 0, right_low, 2 * ROWS, core * (BOX + OWN), TO_LEFT),
    )
    for inside, swap, offset, start, (near, far) in sides:
        for depth, row in enumerate(near + far):
            count = jnp.int32(0)
            for slot in range(SLOTS):
                at = (offset + row) * SLOTS + slot
                column = slot ^ (2 * swap)
                value = jnp.where(inside, inner[row, column], outer[row, column]) - first
                place[at] = value
                if depth < 3:
                    spot[at] = start + depth * SLOTS + slot
                else:
                    wanted = value <= 14 if offset else value >= 3
                    found = start + NEAR + FAR[depth - 3] + count
                    spot[at] = jnp.where(wanted, found, ZERO)
                    count = count + wanted.astype(jnp.int32)

    def fill(row, carry):
        here = jnp.where(row < 6, row + 6, jnp.where(row < 9, row - 3, row + 3)) * SLOTS
        lists = [place[here + n] for n in range(SLOTS)]
        for t in range(SLOTS):
            inside = (lists[t] >= 0) & (lists[t] < 3 * ROWS)
            there = jnp.clip(lists[t], 0, 3 * ROWS - 1) * SLOTS
            found = [(place[there + u], spot[there + u]) for u in range(SLOTS)]
            for s in range(SLOTS):
                index = jnp.int32(ZERO)
                for column, block in found:
                    index = jnp.where(inside & (column == lists[s]), block, index)
                table[row * TAB + s * SLOTS + t] = index
            table[row * TAB + SLOTS * SLOTS + t] = spot[here + t]
        return carry

    lax.fori_loop(0, 2 * ROWS, fill, 0)


def bracket(table, row, operator, term, inverse):
    at = lambda n: table[row * TAB + n]
    mine = [at(SLOTS * SLOTS + t) for t in range(SLOTS)]
    pick = [[at(s * SLOTS + t) for s in range(SLOTS)] for t in range(SLOTS)]
    wide = lambda ref, places: jnp.concatenate([ref[n] for n in places], axis=1)
    left = jnp.concatenate([wide(operator, mine), -wide(term, mine)], axis=1)
    right = jnp.concatenate([wide(ref, p) for ref in (term, operator) for p in pick], axis=0)
    fresh = jnp.dot(left, right, preferred_element_type=jnp.float32)
    fresh = (fresh * inverse).astype(jnp.bfloat16)
    return mine, [fresh[:, s * BLOCK : (s + 1) * BLOCK] for s in range(SLOTS)]


def send_blocks(pack, source, to_inner, to_outer):
    for n in range(BOX):
        to_inner[n] = source[pack[n]]
        to_outer[n] = source[pack[BOX + n]]


def assemble(choose, pack, *refs):
    if choose:
        here, kept, turned_in, own, to_inner, to_outer = refs

        @pl.when(pack[2 * BOX + 1] == 1)
        def _():
            own[0:HALF] = here[...]

        @pl.when(pack[2 * BOX + 1] == 0)
        def _():
            own[0:HALF] = kept[...]

    else:
        kept, turned_in, own, to_inner, to_outer = refs
        own[0:HALF] = kept[...]
    own[HALF:OWN] = turned_in[...]
    send_blocks(pack, own, to_inner, to_outer)


def two_orders(order, last, table, pack, operator, own, inner, outer, *rest):
    if last:
        even_sum, odd_sum, kept, moved, term, first = rest
    else:
        first_out, second_out, to_inner, to_outer, term, first = rest
    zero = jnp.zeros((BLOCK, BLOCK), jnp.bfloat16)
    term[0:BOX] = inner[...]
    term[BOX : BOX + OWN] = own[...]
    term[BOX + OWN : ZERO] = outer[...]
    term[ZERO] = zero
    first[ZERO] = zero

    def first_row(row, carry):
        mine, blocks = bracket(table, row, operator, term, 1.0 / order)
        for n, block in zip(mine, blocks):
            first[n] = block
        return carry

    lax.fori_loop(0, 2 * ROWS, first_row, 0, unroll=UNROLL)

    if not last:
        first_out[...] = first[BOX : BOX + OWN]

    def second_row(row, carry):
        mine, blocks = bracket(table, row, operator, first, 1.0 / (order + 1))
        for n, block in zip(mine, blocks):
            if last:
                term[n] = block
            else:
                second_out[n - BOX] = block
        return carry

    lax.fori_loop(0, ROWS, second_row, 0, unroll=ROWS)

    if not last:
        send_blocks(pack, second_out, to_inner, to_outer)
    else:
        chain = pack[2 * BOX]
        sign = jnp.where(chain == 0, -1.0, 1.0).astype(jnp.float32)

        def join(n, carry):
            for half, out in ((0, kept), (1, moved)):
                at = half * HALF + n
                even = even_sum[at] + WEIGHT[order + 1] * term[BOX + at].astype(jnp.float32)
                odd = odd_sum[at] + WEIGHT[order] * first[BOX + at].astype(jnp.float32)
                out[chain * HALF + n] = even.astype(jnp.bfloat16)
                out[(1 - chain) * HALF + n] = (sign * odd).astype(jnp.bfloat16)
            return carry

        lax.fori_loop(0, HALF, join, 0, unroll=4)


VMEM = pl.BlockSpec(memory_space=pltpu.VMEM)
SMEM = pl.BlockSpec(memory_space=pltpu.SMEM)


def blocks_of(count):
    return jax.ShapeDtypeStruct((count, BLOCK, BLOCK), jnp.bfloat16)


def run_pack(own):
    return pl.pallas_call(
        make_pack,
        out_shape=jax.ShapeDtypeStruct((2 * BOX + 3,), jnp.int32),
        in_specs=[SMEM],
        out_specs=SMEM,
        cost_estimate=pl.CostEstimate(flops=10**6, bytes_accessed=1024, transcendentals=0),
        name="make_pack",
    )(own)


def run_table(left, own, right):
    return pl.pallas_call(
        make_table,
        out_shape=jax.ShapeDtypeStruct((2 * ROWS * TAB,), jnp.int32),
        in_specs=[SMEM] * 3,
        out_specs=SMEM,
        scratch_shapes=[pltpu.SMEM((3 * ROWS * SLOTS,), jnp.int32)] * 2,
        cost_estimate=pl.CostEstimate(flops=10**6, bytes_accessed=1024, transcendentals=0),
        name="make_table",
    )(left, own, right)


def run_assemble(choose, pack, *pieces):
    return pl.pallas_call(
        functools.partial(assemble, choose),
        out_shape=(blocks_of(OWN), blocks_of(BOX), blocks_of(BOX)),
        in_specs=[SMEM] + [VMEM] * len(pieces),
        out_specs=(VMEM,) * 3,
        compiler_params=pltpu.CompilerParams(vmem_limit_bytes=16 * 1024 * 1024),
        cost_estimate=pl.CostEstimate(flops=0, bytes_accessed=3 * 2**20, transcendentals=0),
        name="assemble",
    )(pack, *pieces)


def run_orders(order, last, table, pack, operator, own, inner, outer, sums=()):
    sizes = (OWN, OWN) if last else (OWN, OWN, BOX, BOX)
    return pl.pallas_call(
        functools.partial(two_orders, order, last),
        out_shape=tuple(blocks_of(size) for size in sizes),
        in_specs=[SMEM] * 2 + [VMEM] * (4 + len(sums)),
        out_specs=(VMEM,) * len(sizes),
        scratch_shapes=[pltpu.VMEM((ZERO + 1, BLOCK, BLOCK), jnp.bfloat16)] * 2,
        compiler_params=pltpu.CompilerParams(vmem_limit_bytes=32 * 1024 * 1024),
        cost_estimate=pl.CostEstimate(
            flops=18 * 2 * 2 * 128 * 512 * 512, bytes_accessed=6 * 2**20, transcendentals=0
        ),
        name="two_orders",
    )(table, pack, operator, own, inner, outer, *sums)


def shards(groups, density, hamiltonian, neighbours):
    route = routes(groups)
    _, chain, _, low, odd, _, _ = whereabouts()
    move = functools.partial(lax.ppermute, axis_name=AXES)

    own_h = hamiltonian.reshape(HALF, BLOCK, BLOCK)
    own_lists = move(neighbours, perm=route["turn"])
    turn_part = chain ^ low ^ 1 ^ odd
    own_h, own_lists, turn_part = lax.optimization_barrier((own_h, own_lists, turn_part))
    first_side = move(own_lists, perm=route["inner"])
    second_side = move(own_lists, perm=route["outer"])
    turn_h = move(own_h, perm=route["turn"])
    keep_h = move(own_h, perm=route["keep"])
    turn_x = lax.dynamic_index_in_dim(density, turn_part, 0, False).reshape(HALF, BLOCK, BLOCK)
    here_x = lax.dynamic_index_in_dim(density, 1 - turn_part, 0, False).reshape(HALF, BLOCK, BLOCK)
    keep_x = move(here_x, perm=route["relay"])
    turn_x = move(turn_x, perm=route["turn"])
    keep_x = move(keep_x, perm=route["relay"])

    pack = run_pack(own_lists)
    operator, to_inner, to_outer = run_assemble(False, pack, keep_h, turn_h)
    table = run_table(first_side, own_lists, second_side)
    term, term_inner, term_outer = run_assemble(True, pack, here_x, keep_x, turn_x)
    to_inner, to_outer, term_inner, term_outer, first_side, second_side = lax.optimization_barrier(
        (to_inner, to_outer, term_inner, term_outer, first_side, second_side)
    )
    outer = move(to_outer, perm=route["outer"])
    inner = move(to_inner, perm=route["inner"])
    zero = jnp.zeros((1, BLOCK, BLOCK), jnp.bfloat16)
    operator = jnp.concatenate([inner, operator, outer, zero], axis=0)

    to_inner, to_outer = term_inner, term_outer
    sums = [term.astype(jnp.float32) * WEIGHT[0], jnp.zeros((), jnp.float32)]
    count = STEPS * ORDERS
    for order in range(1, count, 2):
        outer = move(to_outer, perm=route["outer"])
        inner = move(to_inner, perm=route["inner"])
        if order + 1 == count:
            break
        first, term, to_inner, to_outer = run_orders(
            order, False, table, pack, operator, term, inner, outer
        )
        sums[1] = sums[1] + WEIGHT[order] * first.astype(jnp.float32)
        sums[0] = sums[0] + WEIGHT[order + 1] * term.astype(jnp.float32)
    kept, moved = run_orders(
        count - 1, True, table, pack, operator, term, inner, outer, tuple(sums)
    )
    kept = move(kept, perm=route["keep_back"])
    moved = move(moved, perm=route["turn_back"])
    total = kept.astype(jnp.float32) + moved.astype(jnp.float32)
    return total.reshape(density.shape)


def solution(mesh):
    placed = (P(None, "dom", "col", None, None), P("dom", "col", None, None), P("dom", None))
    return jax.shard_map(
        functools.partial(shards, mesh.shape["dom"] // 4),
        mesh=mesh,
        in_specs=placed,
        out_specs=P(None, "dom", "col", None, None),
        check_vma=False,
    )
```
